32 devices in a mesh: batch: 16 (over z, x, core), crop: 2 (over y).
Axes of the slice: x: 2, y: 2, z: 4, core: 2. Of those that a mesh axis runs over, the one named last changes fastest.
Arguments:
- voxels: bfloat16 [2, 16384, 512], P('crop', 'batch'), may hold values from -6 to 6
- phrases: bfloat16 [256, 512], P('batch'), may hold values from -6 to 6
- pair_ids: int32 [256], P('batch'), may hold values from 0 to 63
- margin_index: int32 [2, 16, 512], P('crop', 'batch'), may hold values from 0 to 1023, as said below
Outputs:
- voxel_grad: float32 [2, 16384, 512], P('crop', 'batch')
- phrase_grad: float32 [256, 512], P('batch')
The draws below stay inside these ranges and needn't reach their ends.
Inputs may be any that keep to these rules, and one draw needn't show every extreme that they name: Each list margin_index[c, b] holds 512 distinct rows of that batch index's 1024 rows; entry k of crop 0 and entry k of crop 1 at the same b show the same place.
All inputs are finite; a program needn't handle non-finite values.
Results may differ from the reference program's by a relative error of at most 0.0013.
Values may be sent and summed in bfloat16 or wider, within the bound.
No kernel may reach another device: no remote copies, remote signals or barrier semaphores. Data moves between devices by JAX's collectives and lax.ppermute only.
A program may use at most 64 MiB of HBM per device.

```python
import math
import jax
import jax.numpy as jnp
from jax import lax

D = 512
VOX_DEV = 1024
VOX_VOL = 256
OVL = 512
VOXELS = 16384
PHRASES = 256
VOLUMES = 64
N_BATCH = 16


def draw_margin_index(key, part):
    keys = jax.random.split(key, 2 * N_BATCH)

    def one_list(single):
        return jax.random.permutation(single, VOX_DEV)[:OVL].astype(jnp.int32)
    lists = jax.vmap(one_list)(keys)
    return lists.reshape(2, N_BATCH, OVL)


def set_ends(entries, own_key, least, top_value):
    shape = entries.shape
    index_at = [jax.random.randint(jax.random.fold_in(own_key, axis), (), 0, shape[axis]) for axis in range(len(shape))]
    entries = entries.at[tuple(index_at)].set(least)
    longest = shape.index(max(shape))
    index_at[longest] = (index_at[longest] + 1) % shape[longest]
    return entries.at[tuple(index_at)].set(top_value)


def block_levels(key, extent, cuts, least, high):
    level, own = 1.0, jax.random.fold_in(key, 6)
    for dim, shards_of in cuts:
        draws = jnp.exp(jax.random.uniform(jax.random.fold_in(own, dim), (shards_of,), jnp.float32, least / len(cuts), high / len(cuts)))
        level = level * jnp.repeat(draws, extent[dim] // shards_of).reshape([-1 if axis == dim else 1 for axis in range(len(extent))])
    return level


def gaussian(key, shape, spread, bound, cuts=(), held_as=jnp.bfloat16):
    gain = block_levels(key, shape, cuts, -0.22, 0.18) if cuts else 1.0
    result = jax.random.normal(key, shape, jnp.float32) * spread * gain
    return jnp.minimum(jnp.maximum(result, -bound), bound).astype(held_as)


def setup_inputs(seed: int = 0) -> dict:
    key_list = jax.random.split(jax.random.key(seed), 5)
    return {
        "voxels": gaussian(key_list[0], (2, VOXELS, D), 1.0, 6.0, ((0, 2), (1, 16))),
        "phrases": gaussian(key_list[1], (PHRASES, D), 1.0, 6.0, ((0, 16),)),
        "pair_ids": set_ends(jax.random.randint(key_list[2], (PHRASES,), 0, VOLUMES), jax.random.fold_in(key_list[2], 1), 0, VOLUMES - 1).astype(jnp.int32),
        "margin_index": draw_margin_index(jax.random.fold_in(key_list[4], 71), 0),
    }


def reference(voxels, phrases, pair_ids, margin_index):
    scale = 1.0 / math.sqrt(D)
    all_rows = voxels.reshape(2 * VOXELS, D)
    block_rows = math.gcd(2 * VOXELS, 2048)
    num_blocks = 2 * VOXELS // block_rows
    blocks = all_rows.reshape(num_blocks, block_rows, D)
    starts = jnp.arange(num_blocks, dtype=jnp.int32) * block_rows

    def one_block(total, pieces):
        group, start = pieces
        index = start + jnp.arange(block_rows, dtype=jnp.int32)
        volume = index % VOXELS // VOX_VOL
        sign = jnp.where(volume[:, None] == pair_ids[None, :], 1.0, -1.0).astype(jnp.float32)
        logit = jnp.dot(group, phrases.T, preferred_element_type=jnp.float32) * scale - 1.0
        dlogit = (-sign * jax.nn.sigmoid(-sign * logit)).astype(jnp.bfloat16)
        match_part = jnp.dot(dlogit, phrases, preferred_element_type=jnp.float32) * scale
        phrase_part = jnp.dot(dlogit.T, group, preferred_element_type=jnp.float32) * scale
        return (total + phrase_part, match_part)
    phrase_grad, match_blocks = lax.scan(one_block, jnp.zeros((PHRASES, D), jnp.float32), (blocks, starts))
    match_grad = match_blocks.reshape(2, VOXELS, D)
    base = (jnp.arange(N_BATCH, dtype=jnp.int32) * VOX_DEV)[:, None]
    rows_first = (base + margin_index[0].astype(jnp.int32)).reshape(-1)
    rows_second = (base + margin_index[1].astype(jnp.int32)).reshape(-1)
    first = voxels[0][rows_first].astype(jnp.float32)
    second = voxels[1][rows_second].astype(jnp.float32)
    diff = first - second
    grad_first = match_grad[0].at[rows_first].add(diff)
    grad_second = match_grad[1].at[rows_second].add(-diff)
    voxel_grad = jnp.stack([grad_first, grad_second])
    return (voxel_grad, phrase_grad)
```

```python
import functools
import math

import jax
import jax.numpy as jnp
from jax import lax
from jax.experimental import pallas as pl
from jax.experimental.pallas import tpu as pltpu
from jax.sharding import PartitionSpec as P

VOX_VOL = 256
VOL_SHIFT = VOX_VOL.bit_length() - 1
LANES = 128
VMEM_LIMIT = 24 * 1024 * 1024

F32 = jnp.float32
BF16 = jnp.bfloat16


def vmem_spec():
    return pl.BlockSpec(memory_space=pltpu.VMEM)


def pack_kernel(copies, ids_ref, phrases_ref, out_ref):
    rows, width = phrases_ref.shape
    row = lax.broadcasted_iota(jnp.int32, (rows, LANES), 0)
    lane = lax.broadcasted_iota(jnp.int32, (rows, LANES), 1)
    ids = jnp.zeros((rows, LANES), jnp.int32)
    for i in range(rows):
        ids = jnp.where(row == i, ids_ref[i], ids)
    parts = jnp.where(lane == 0, ids >> 8, jnp.where(lane == 1, ids & 255, 0))
    parts = parts.astype(F32).astype(BF16)
    phrases = phrases_ref[...]

    def put(i):
        out_ref[pl.ds(pl.multiple_of(i * rows, rows), rows), :width] = phrases
        out_ref[pl.ds(pl.multiple_of(i * rows, rows), rows), width:] = parts

    if copies <= 16:
        for i in range(copies):
            put(i)
    else:
        pl.loop(0, copies)(put)


def main_kernel(scale, base_ref, vox_ref, near_ref, far_ref, idx_ref, dl_ref, near_out, far_out, chosen_ref):
    rows, width = vox_ref.shape
    half = near_ref.shape[0]
    block = min(half, 128)
    volume = (base_ref[0] + lax.broadcasted_iota(jnp.int32, (1, rows), 1)) >> VOL_SHIFT
    volume = volume.astype(F32)

    def terms(src_ref, out_ref, offset, start):
        at = pl.ds(pl.multiple_of(start, block), block)
        phrases = src_ref[at, :width]
        parts = src_ref[at, width:].astype(F32)
        ids = parts[:, 0:1] * 256.0 + parts[:, 1:2]
        logit = lax.dot_general(
            phrases, vox_ref[...], (((1,), (1,)), ((), ())), preferred_element_type=F32
        )
        sign = jnp.where(ids == volume, 1.0, -1.0).astype(F32)
        dlogit = (-sign / (1.0 + jnp.exp(sign * (logit * scale - 1.0)))).astype(BF16)
        dl_ref[pl.ds(pl.multiple_of(offset + start, block), block), :] = dlogit
        out_ref[at, :] = jnp.dot(dlogit, vox_ref[...], preferred_element_type=F32) * scale

    for src_ref, out_ref, offset in ((far_ref, far_out, half), (near_ref, near_out, 0)):
        if half == block:
            terms(src_ref, out_ref, offset, 0)
        else:
            pl.loop(0, half // block)(
                lambda j, s=src_ref, o=out_ref, f=offset: terms(s, o, f, j * block)
            )

    picks = idx_ref.shape[1]
    column = jnp.broadcast_to(idx_ref[...], (8, picks)).T[:, 0:1]
    onehot = (column == lax.broadcasted_iota(jnp.int32, (picks, rows), 1)).astype(F32).astype(BF16)
    chosen_ref[...] = jnp.dot(onehot, vox_ref[...], preferred_element_type=F32).astype(BF16)


def grad_kernel(scale, idx_ref, vox_ref, partner_ref, dl_ref, near_ref, far_ref, out_ref):
    rows, width = vox_ref.shape
    half = near_ref.shape[0]
    picks = idx_ref.shape[1]
    at = pl.program_id(0) * rows + lax.broadcasted_iota(jnp.int32, (rows, picks), 0)
    spread = (at == idx_ref[...]).astype(F32)
    taken = jnp.sum(spread, axis=1, keepdims=True)
    tn = (((0,), (0,)), ((), ()))
    match = lax.dot_general(dl_ref[:half, :], near_ref[:, :width], tn, preferred_element_type=F32)
    match += lax.dot_general(dl_ref[half:, :], far_ref[:, :width], tn, preferred_element_type=F32)
    other = jnp.dot(spread.astype(BF16), partner_ref[...], preferred_element_type=F32)
    out_ref[...] = match * scale + taken * vox_ref[...].astype(F32) - other


def local(voxels, phrases, pair_ids, margin_index):
    own_vox = voxels[0]
    rows, width = own_vox.shape
    owned = phrases.shape[0]
    picks = margin_index.shape[-1]
    scale = 1.0 / math.sqrt(width)
    devices = lax.axis_size("batch")
    crops = lax.axis_size("crop")
    members = devices // 2
    half = members * owned
    total = 2 * half
    same_core = [[2 * i + core for i in range(members)] for core in range(2)]
    cores = [(i, i ^ 1) for i in range(devices)]
    swap = [(i, i ^ 1) for i in range(crops)]
    params = pltpu.CompilerParams(vmem_limit_bytes=VMEM_LIMIT)

    packed = pl.pallas_call(
        functools.partial(pack_kernel, members),
        out_shape=jax.ShapeDtypeStruct((half, width + LANES), BF16),
        in_specs=[pl.BlockSpec(memory_space=pltpu.SMEM), vmem_spec()],
        out_specs=vmem_spec(),
        compiler_params=params,
        name="pack",
    )(pair_ids, phrases)
    near = lax.all_to_all(packed, "batch", 0, 0, tiled=True, axis_index_groups=same_core)
    far = lax.ppermute(near, "batch", cores)

    picked = margin_index[0]
    base = (lax.axis_index("batch") * rows).astype(jnp.int32).reshape(1)
    dlogit, near_terms, far_terms, chosen = pl.pallas_call(
        functools.partial(main_kernel, scale),
        out_shape=[
            jax.ShapeDtypeStruct((total, rows), BF16),
            jax.ShapeDtypeStruct((half, width), F32),
            jax.ShapeDtypeStruct((half, width), F32),
            jax.ShapeDtypeStruct((picks, width), BF16),
        ],
        in_specs=[pl.BlockSpec(memory_space=pltpu.SMEM)] + [vmem_spec()] * 4,
        out_specs=[vmem_spec()] * 4,
        compiler_params=params,
        cost_estimate=pl.CostEstimate(
            flops=4 * total * rows * width + 2 * picks * rows * width,
            bytes_accessed=4 * rows * width,
            transcendentals=total * rows,
        ),
        name="terms",
    )(base, own_vox, near, far, picked)

    from_core = lax.ppermute(far_terms, "batch", cores)
    partner = lax.ppermute(chosen, "crop", swap)
    pieces = lax.all_to_all(
        near_terms + from_core, "batch", 0, 0, tiled=True, axis_index_groups=same_core
    )
    own = jnp.sum(pieces.reshape(members, owned, width), axis=0)
    own, partner = lax.optimization_barrier((own, partner))
    phrase_grad = own + lax.ppermute(own, "crop", swap)

    block = math.gcd(rows, 256)
    voxel_grad = pl.pallas_call(
        functools.partial(grad_kernel, scale),
        out_shape=jax.ShapeDtypeStruct((rows, width), F32),
        grid=(rows // block,),
        in_specs=[
            pl.BlockSpec((1, picks), lambda i: (0, 0)),
            pl.BlockSpec((block, width), lambda i: (i, 0)),
            pl.BlockSpec((picks, width), lambda i: (0, 0)),
            pl.BlockSpec((total, block), lambda i: (0, i)),
            pl.BlockSpec((half, width + LANES), lambda i: (0, 0)),
            pl.BlockSpec((half, width + LANES), lambda i: (0, 0)),
        ],
        out_specs=pl.BlockSpec((block, width), lambda i: (i, 0)),
        compiler_params=params,
        cost_estimate=pl.CostEstimate(
            flops=2 * total * rows * width + 2 * picks * rows * width,
            bytes_accessed=8 * rows * width,
            transcendentals=0,
        ),
        name="voxel_grad",
    )(picked, own_vox, partner, dlogit, near, far)
    return (voxel_grad[None], phrase_grad)


def solution(mesh):
    placed = (P("crop", "batch", None), P("batch", None), P("batch"), P("crop", "batch", None))
    return jax.shard_map(
        local,
        mesh=mesh,
        in_specs=placed,
        out_specs=(P("crop", "batch", None), P("batch", None)),
        check_vma=False,
    )
```

```python
import functools
import math

import jax
import jax.numpy as jnp
from jax import lax
from jax.experimental import pallas as pl
from jax.experimental.pallas import tpu as pltpu
from jax.sharding import PartitionSpec as P

VOX_VOL = 256
VOL_SHIFT = VOX_VOL.bit_length() - 1
LANES = 128
VMEM_LIMIT = 24 * 1024 * 1024

F32 = jnp.float32
BF16 = jnp.bfloat16


def vmem_spec():
    return pl.BlockSpec(memory_space=pltpu.VMEM)


def pack_kernel(copies, ids_hbm, phrases_hbm, out_ref, ids_ref, phrases_ref, sems):
    rows, width = phrases_ref.shape
    get_ids = pltpu.make_async_copy(ids_hbm, ids_ref, sems.at[0])
    get_phrases = pltpu.make_async_copy(phrases_hbm, phrases_ref, sems.at[1])
    get_ids.start()
    get_phrases.start()
    row = lax.broadcasted_iota(jnp.int32, (rows, LANES), 0)
    lane = lax.broadcasted_iota(jnp.int32, (rows, LANES), 1)
    get_ids.wait()
    ids = jnp.zeros((rows, LANES), jnp.int32)
    for i in range(rows):
        ids = jnp.where(row == i, ids_ref[i], ids)
    parts = jnp.where(lane == 0, ids >> 8, jnp.where(lane == 1, ids & 255, 0))
    parts = parts.astype(F32).astype(BF16)
    get_phrases.wait()
    phrases = phrases_ref[...]

    def put(i):
        out_ref[pl.ds(pl.multiple_of(i * rows, rows), rows), :width] = phrases
        out_ref[pl.ds(pl.multiple_of(i * rows, rows), rows), width:] = parts

    if copies <= 16:
        for i in range(copies):
            put(i)
    else:
        pl.loop(0, copies)(put)


def margin_kernel(vox_ref, idx_ref, chosen_ref):
    rows = vox_ref.shape[0]
    picks = idx_ref.shape[1]
    column = jnp.broadcast_to(idx_ref[...], (8, picks)).T[:, 0:1]
    onehot = (column == lax.broadcasted_iota(jnp.int32, (picks, rows), 1)).astype(F32).astype(BF16)
    chosen_ref[...] = jnp.dot(onehot, vox_ref[...], preferred_element_type=F32).astype(BF16)


def terms_kernel(scale, base_ref, vox_ref, packed_ref, dl_ref, out_ref):
    rows, width = vox_ref.shape
    half = packed_ref.shape[0]
    block = min(half, 128)
    volume = (base_ref[0] + lax.broadcasted_iota(jnp.int32, (1, rows), 1)) >> VOL_SHIFT
    volume = volume.astype(F32)

    def terms(start):
        at = pl.ds(pl.multiple_of(start, block), block)
        phrases = packed_ref[at, :width]
        parts = packed_ref[at, width:].astype(F32)
        ids = parts[:, 0:1] * 256.0 + parts[:, 1:2]
        logit = lax.dot_general(
            phrases, vox_ref[...], (((1,), (1,)), ((), ())), preferred_element_type=F32
        )
        sign = jnp.where(ids == volume, 1.0, -1.0).astype(F32)
        dlogit = (-sign / (1.0 + jnp.exp(sign * (logit * scale - 1.0)))).astype(BF16)
        dl_ref[at, :] = dlogit
        out_ref[at, :] = jnp.dot(dlogit, vox_ref[...], preferred_element_type=F32) * scale

    if half == block:
        terms(0)
    else:
        pl.loop(0, half // block)(lambda j: terms(j * block))


def grad_kernel(
    scale, block, idx_ref, vox_ref, partner_ref, dl_near, dl_far, near_ref, far_ref, out_hbm, out_ref, sems
):
    rows, width = vox_ref.shape
    picks = idx_ref.shape[1]
    tn = (((0,), (0,)), ((), ()))
    copies = []
    for i in range(rows // block):
        at = pl.ds(i * block, block)
        row = i * block + lax.broadcasted_iota(jnp.int32, (block, picks), 0)
        spread = (row == idx_ref[...]).astype(F32)
        taken = jnp.sum(spread, axis=1, keepdims=True)
        match = lax.dot_general(
            dl_near[:, at], near_ref[:, :width], tn, preferred_element_type=F32
        ) + lax.dot_general(dl_far[:, at], far_ref[:, :width], tn, preferred_element_type=F32)
        other = jnp.dot(spread.astype(BF16), partner_ref[...], preferred_element_type=F32)
        out_ref[at, :] = match * scale + taken * vox_ref[at, :].astype(F32) - other
        copies.append(pltpu.make_async_copy(out_ref.at[at, :], out_hbm.at[at, :], sems.at[i]))
        copies[-1].start()
    for copy in copies:
        copy.wait()


def local(voxels, phrases, pair_ids, margin_index):
    own_vox = voxels[0]
    rows, width = own_vox.shape
    owned = phrases.shape[0]
    picks = margin_index.shape[-1]
    scale = 1.0 / math.sqrt(width)
    devices = lax.axis_size("batch")
    crops = lax.axis_size("crop")
    members = devices // 2
    half = members * owned
    same_core = [[2 * i + core for i in range(members)] for core in range(2)]
    cores = [(i, i ^ 1) for i in range(devices)]
    swap = [(i, i ^ 1) for i in range(crops)]
    params = pltpu.CompilerParams(vmem_limit_bytes=VMEM_LIMIT)
    smem = pl.BlockSpec(memory_space=pltpu.SMEM)
    hbm = pl.BlockSpec(memory_space=pltpu.HBM)

    lane = lax.broadcasted_iota(jnp.int32, (owned, LANES), 1)
    id_parts = jnp.where(lane == 0, pair_ids[:, None] >> 8, pair_ids[:, None] & 255)
    id_parts = id_parts.astype(BF16)
    own_block = jnp.concatenate([phrases, id_parts], axis=1)
    packed = jnp.broadcast_to(own_block[None], (members, owned, width + LANES)).reshape(half, width + LANES)
    near = lax.all_to_all(packed, "batch", 0, 0, tiled=True, axis_index_groups=same_core)
    far = lax.ppermute(near, "batch", cores)

    picked = margin_index[0]
    chosen = pl.pallas_call(
        margin_kernel,
        out_shape=jax.ShapeDtypeStruct((picks, width), BF16),
        in_specs=[vmem_spec()] * 2,
        out_specs=vmem_spec(),
        compiler_params=params,
        cost_estimate=pl.CostEstimate(
            flops=2 * picks * rows * width, bytes_accessed=2 * rows * width, transcendentals=0
        ),
        name="margin_rows",
    )(own_vox, picked)

    base = (lax.axis_index("batch") * rows).astype(jnp.int32).reshape(1)
    terms = pl.pallas_call(
        functools.partial(terms_kernel, scale),
        out_shape=[
            jax.ShapeDtypeStruct((half, rows), BF16),
            jax.ShapeDtypeStruct((half, width), F32),
        ],
        in_specs=[smem] + [vmem_spec()] * 2,
        out_specs=[vmem_spec()] * 2,
        compiler_params=params,
        cost_estimate=pl.CostEstimate(
            flops=4 * half * rows * width,
            bytes_accessed=2 * rows * width,
            transcendentals=half * rows,
        ),
        name="terms",
    )
    far, chosen = lax.optimization_barrier((far, chosen))
    partner = lax.ppermute(chosen, "crop", swap)
    dl_far, far_terms = terms(base, own_vox, far)
    from_core = lax.ppermute(far_terms, "batch", cores)
    dl_near, near_terms = terms(base, own_vox, near)

    pieces = lax.all_to_all(
        near_terms + from_core, "batch", 0, 0, tiled=True, axis_index_groups=same_core
    )
    own = jnp.sum(pieces.reshape(members, owned, width), axis=0)
    own, partner = lax.optimization_barrier((own, partner))
    phrase_grad = own + lax.ppermute(own, "crop", swap)

    block = math.gcd(rows, 256)
    voxel_grad = pl.pallas_call(
        functools.partial(grad_kernel, scale, block),
        out_shape=jax.ShapeDtypeStruct((rows, width), F32),
        in_specs=[vmem_spec()] * 7,
        out_specs=hbm,
        scratch_shapes=[pltpu.VMEM((rows, width), F32), pltpu.SemaphoreType.DMA((rows // block,))],
        compiler_params=params,
        cost_estimate=pl.CostEstimate(
            flops=4 * half * rows * width + 2 * picks * rows * width,
            bytes_accessed=8 * rows * width,
            transcendentals=0,
        ),
        name="voxel_grad",
    )(picked, own_vox, partner, dl_near, dl_far, near, far)
    return (voxel_grad[None], phrase_grad)


def solution(mesh):
    placed = (P("crop", "batch", None), P("batch", None), P("batch"), P("crop", "batch", None))
    return jax.shard_map(
        local,
        mesh=mesh,
        in_specs=placed,
        out_specs=(P("crop", "batch", None), P("batch", None)),
        check_vma=False,
    )
```

```python
import functools
import math

import jax
import jax.numpy as jnp
from jax import lax
from jax.experimental import pallas as pl
from jax.experimental.pallas import tpu as pltpu
from jax.sharding import PartitionSpec as P

VOX_VOL = 256
VOL_SHIFT = VOX_VOL.bit_length() - 1
LANES = 128
VMEM_LIMIT = 24 * 1024 * 1024

F32 = jnp.float32
BF16 = jnp.bfloat16


def vmem_spec():
    return pl.BlockSpec(memory_space=pltpu.VMEM)


def cells_kernel(owned, ids_ref, out_ref):
    row = lax.broadcasted_iota(jnp.int32, out_ref.shape, 0)
    lane = lax.broadcasted_iota(jnp.int32, out_ref.shape, 1)
    ids = ids_ref[...]
    cells = jnp.where(lane == row, ids >> 8, jnp.where(lane == row + owned, ids & 255, 0))
    out_ref[...] = cells.astype(F32).astype(BF16)


def repeat_kernel(copies, phrases_ref, cells_ref, out_ref):
    rows, width = phrases_ref.shape
    phrases, cells = phrases_ref[...], cells_ref[...]

    def put(i):
        at = pl.ds(pl.multiple_of(i * rows, rows), rows)
        out_ref[at, :width] = phrases
        out_ref[at, width:] = cells

    if copies <= 16:
        for i in range(copies):
            put(i)
    else:
        pl.loop(0, copies)(put)


def margin_kernel(vox_ref, idx_ref, chosen_ref):
    rows = vox_ref.shape[0]
    picks = idx_ref.shape[1]
    column = jnp.broadcast_to(idx_ref[...], (8, picks)).T[:, 0:1]
    onehot = (column == lax.broadcasted_iota(jnp.int32, (picks, rows), 1)).astype(F32).astype(BF16)
    chosen_ref[...] = jnp.dot(onehot, vox_ref[...], preferred_element_type=F32).astype(BF16)


def terms_kernel(scale, owned, base_ref, vox_ref, packed_ref, dl_ref, out_ref):
    rows, width = vox_ref.shape
    half = packed_ref.shape[0]
    block = min(half, 128)
    volume = (base_ref[0] + lax.broadcasted_iota(jnp.int32, (1, rows), 1)) >> VOL_SHIFT
    volume = volume.astype(F32)

    def terms(start):
        at = pl.ds(pl.multiple_of(start, block), block)
        phrases = packed_ref[at, :width]
        cells = packed_ref[at, width:].astype(F32)
        lane = lax.broadcasted_iota(jnp.int32, cells.shape, 1)
        ids = jnp.sum(jnp.where(lane < owned, cells * 256.0, cells), axis=1, keepdims=True)
        logit = lax.dot_general(
            phrases, vox_ref[...], (((1,), (1,)), ((), ())), preferred_element_type=F32
        )
        sign = jnp.where(ids == volume, 1.0, -1.0).astype(F32)
        dlogit = (-sign / (1.0 + jnp.exp(sign * (logit * scale - 1.0)))).astype(BF16)
        dl_ref[at, :] = dlogit
        out_ref[at, :] = jnp.dot(dlogit, vox_ref[...], preferred_element_type=F32) * scale

    if half == block:
        terms(0)
    else:
        pl.loop(0, half // block)(lambda j: terms(j * block))


def grad_kernel(
    scale, block, idx_ref, vox_ref, partner_ref, dl_near, dl_far, near_ref, far_ref, out_hbm, out_ref, sems
):
    rows, width = vox_ref.shape
    picks = idx_ref.shape[1]
    tn = (((0,), (0,)), ((), ()))
    copies = []
    for i in range(rows // block):
        at = pl.ds(i * block, block)
        row = i * block + lax.broadcasted_iota(jnp.int32, (block, picks), 0)
        spread = (row == idx_ref[...]).astype(F32)
        taken = jnp.sum(spread, axis=1, keepdims=True)
        match = lax.dot_general(
            dl_near[:, at], near_ref[:, :width], tn, preferred_element_type=F32
        ) + lax.dot_general(dl_far[:, at], far_ref[:, :width], tn, preferred_element_type=F32)
        other = jnp.dot(spread.astype(BF16), partner_ref[...], preferred_element_type=F32)
        out_ref[at, :] = match * scale + taken * vox_ref[at, :].astype(F32) - other
        copies.append(pltpu.make_async_copy(out_ref.at[at, :], out_hbm.at[at, :], sems.at[i]))
        copies[-1].start()
    for copy in copies:
        copy.wait()


def local(voxels, phrases, pair_ids, margin_index):
    own_vox = voxels[0]
    rows, width = own_vox.shape
    owned = phrases.shape[0]
    picks = margin_index.shape[-1]
    scale = 1.0 / math.sqrt(width)
    devices = lax.axis_size("batch")
    crops = lax.axis_size("crop")
    members = devices // 2
    half = members * owned
    same_core = [[2 * i + core for i in range(members)] for core in range(2)]
    cores = [(i, i ^ 1) for i in range(devices)]
    swap = [(i, i ^ 1) for i in range(crops)]
    params = pltpu.CompilerParams(vmem_limit_bytes=VMEM_LIMIT)
    smem = pl.BlockSpec(memory_space=pltpu.SMEM)
    hbm = pl.BlockSpec(memory_space=pltpu.HBM)

    cells = pl.pallas_call(
        functools.partial(cells_kernel, owned),
        out_shape=jax.ShapeDtypeStruct((owned, LANES), BF16),
        in_specs=[vmem_spec()],
        out_specs=vmem_spec(),
        compiler_params=params,
        cost_estimate=pl.CostEstimate(flops=10**9, bytes_accessed=1024, transcendentals=0),
        name="id_cells",
    )(jnp.pad(jnp.concatenate([pair_ids, pair_ids]), (0, LANES - 2 * owned))[None, :])
    packed = pl.pallas_call(
        functools.partial(repeat_kernel, members),
        out_shape=jax.ShapeDtypeStruct((half, width + LANES), BF16),
        in_specs=[vmem_spec()] * 2,
        out_specs=vmem_spec(),
        compiler_params=params,
        cost_estimate=pl.CostEstimate(flops=10**9, bytes_accessed=1024, transcendentals=0),
        name="repeat",
    )(phrases, cells)
    near = lax.all_to_all(packed, "batch", 0, 0, tiled=True, axis_index_groups=same_core)
    far = lax.ppermute(near, "batch", cores)

    picked = margin_index[0]
    chosen = pl.pallas_call(
        margin_kernel,
        out_shape=jax.ShapeDtypeStruct((picks, width), BF16),
        in_specs=[vmem_spec()] * 2,
        out_specs=vmem_spec(),
        compiler_params=params,
        cost_estimate=pl.CostEstimate(
            flops=2 * picks * rows * width, bytes_accessed=2 * rows * width, transcendentals=0
        ),
        name="margin_rows",
    )(own_vox, picked)

    base = (lax.axis_index("batch") * rows).astype(jnp.int32).reshape(1)
    terms = pl.pallas_call(
        functools.partial(terms_kernel, scale, owned),
        out_shape=[
            jax.ShapeDtypeStruct((half, rows), BF16),
            jax.ShapeDtypeStruct((half, width), F32),
        ],
        in_specs=[smem] + [vmem_spec()] * 2,
        out_specs=[vmem_spec()] * 2,
        compiler_params=params,
        cost_estimate=pl.CostEstimate(
            flops=4 * half * rows * width,
            bytes_accessed=2 * rows * width,
            transcendentals=half * rows,
        ),
        name="terms",
    )
    far, chosen = lax.optimization_barrier((far, chosen))
    partner = lax.ppermute(chosen, "crop", swap)
    dl_far, far_terms = terms(base, own_vox, far)
    from_core = lax.ppermute(far_terms, "batch", cores)
    dl_near, near_terms = terms(base, own_vox, near)

    pieces = lax.all_to_all(
        near_terms + from_core, "batch", 0, 0, tiled=True, axis_index_groups=same_core
    )
    own = jnp.sum(pieces.reshape(members, owned, width), axis=0)
    own, partner = lax.optimization_barrier((own, partner))
    phrase_grad = own + lax.ppermute(own, "crop", swap)

    block = math.gcd(rows, 256)
    voxel_grad = pl.pallas_call(
        functools.partial(grad_kernel, scale, block),
        out_shape=jax.ShapeDtypeStruct((rows, width), F32),
        in_specs=[vmem_spec()] * 7,
        out_specs=hbm,
        scratch_shapes=[pltpu.VMEM((rows, width), F32), pltpu.SemaphoreType.DMA((rows // block,))],
        compiler_params=params,
        cost_estimate=pl.CostEstimate(
            flops=4 * half * rows * width + 2 * picks * rows * width,
            bytes_accessed=8 * rows * width,
            transcendentals=0,
        ),
        name="voxel_grad",
    )(picked, own_vox, partner, dl_near, dl_far, near, far)
    return (voxel_grad[None], phrase_grad)


def solution(mesh):
    placed = (P("crop", "batch", None), P("batch", None), P("batch"), P("crop", "batch", None))
    return jax.shard_map(
        local,
        mesh=mesh,
        in_specs=placed,
        out_specs=(P("crop", "batch", None), P("batch", None)),
        check_vma=False,
    )
```

```python
import functools
import math

import jax
import jax.numpy as jnp
from jax import lax
from jax.experimental import pallas as pl
from jax.experimental.pallas import tpu as pltpu
from jax.sharding import PartitionSpec as P

VOX_VOL = 256
VOL_SHIFT = VOX_VOL.bit_length() - 1
LANES = 128
VMEM_LIMIT = 24 * 1024 * 1024

F32 = jnp.float32
BF16 = jnp.bfloat16


def vmem_spec():
    return pl.BlockSpec(memory_space=pltpu.VMEM)


def cells_kernel(owned, ids_ref, out_ref):
    row = lax.broadcasted_iota(jnp.int32, out_ref.shape, 0)
    lane = lax.broadcasted_iota(jnp.int32, out_ref.shape, 1)
    ids = ids_ref[...]
    cells = jnp.where(lane == row, ids >> 8, jnp.where(lane == row + owned, ids & 255, 0))
    out_ref[...] = cells.astype(F32).astype(BF16)


def stack_kernel(*refs):
    out_ref = refs[-1]
    start = 0
    for ref in refs[:-1]:
        rows = ref.shape[0]
        out_ref[start : start + rows, :] = ref[...]
        start += rows


def beside_kernel(phrases_ref, cells_ref, out_ref):
    width = phrases_ref.shape[1]
    out_ref[:, :width] = phrases_ref[...]
    out_ref[:, width:] = cells_ref[...]


def margin_kernel(vox_ref, idx_ref, chosen_ref):
    rows = vox_ref.shape[0]
    picks = idx_ref.shape[1]
    onehot = (idx_ref[...] == lax.broadcasted_iota(jnp.int32, (rows, picks), 0)).astype(F32).astype(BF16)
    chosen_ref[...] = lax.dot_general(
        onehot, vox_ref[...], (((0,), (0,)), ((), ())), preferred_element_type=F32
    ).astype(BF16)


def terms_kernel(scale, owned, base_ref, vox_ref, packed_ref, dl_ref, out_ref):
    rows, width = vox_ref.shape
    half = packed_ref.shape[0]
    block = min(half, 128)
    volume = (base_ref[0] + lax.broadcasted_iota(jnp.int32, (1, rows), 1)) >> VOL_SHIFT
    volume = volume.astype(F32)

    def terms(start):
        at = pl.ds(pl.multiple_of(start, block), block)
        phrases = packed_ref[at, :width]
        cells = packed_ref[at, width:].astype(F32)
        lane = lax.broadcasted_iota(jnp.int32, cells.shape, 1)
        ids = jnp.sum(jnp.where(lane < owned, cells * 256.0, cells), axis=1, keepdims=True)
        logit = lax.dot_general(
            phrases, vox_ref[...], (((1,), (1,)), ((), ())), preferred_element_type=F32
        )
        sign = jnp.where(ids == volume, 1.0, -1.0).astype(F32)
        dlogit = (-sign / (1.0 + jnp.exp(sign * (logit * scale - 1.0)))).astype(BF16)
        dl_ref[at, :] = dlogit
        out_ref[at, :] = jnp.dot(dlogit, vox_ref[...], preferred_element_type=F32) * scale

    if half == block:
        terms(0)
    else:
        pl.loop(0, half // block)(lambda j: terms(j * block))


def match_kernel(scale, idx_ref, vox_ref, dl_near, dl_far, near_ref, far_ref, out_ref):
    rows, width = vox_ref.shape
    picks = idx_ref.shape[1]
    block = math.gcd(rows, 256)
    tn = (((0,), (0,)), ((), ()))
    for i in range(rows // block):
        at = pl.ds(i * block, block)
        row = i * block + lax.broadcasted_iota(jnp.int32, (block, picks), 0)
        taken = jnp.sum((row == idx_ref[...]).astype(F32), axis=1, keepdims=True)
        match = lax.dot_general(
            dl_near[:, at], near_ref[:, :width], tn, preferred_element_type=F32
        ) + lax.dot_general(dl_far[:, at], far_ref[:, :width], tn, preferred_element_type=F32)
        out_ref[at, :] = match * scale + taken * vox_ref[at, :].astype(F32)


def grad_kernel(block, idx_ref, part_ref, partner_ref, out_hbm, out_ref, sems):
    rows, width = part_ref.shape
    picks = idx_ref.shape[1]
    copies = []
    for i in range(rows // block):
        at = pl.ds(i * block, block)
        row = i * block + lax.broadcasted_iota(jnp.int32, (block, picks), 0)
        spread = (row == idx_ref[...]).astype(F32).astype(BF16)
        other = jnp.dot(spread, partner_ref[...], preferred_element_type=F32)
        out_ref[at, :] = part_ref[at, :] - other
        copies.append(pltpu.make_async_copy(out_ref.at[at, :], out_hbm.at[at, :], sems.at[i]))
        copies[-1].start()
    for copy in copies:
        copy.wait()


def local(voxels, phrases, pair_ids, margin_index):
    own_vox = voxels[0]
    rows, width = own_vox.shape
    owned = phrases.shape[0]
    picks = margin_index.shape[-1]
    scale = 1.0 / math.sqrt(width)
    devices = lax.axis_size("batch")
    crops = lax.axis_size("crop")
    members = devices // 2
    half = members * owned
    swap = [(i, i ^ 1) for i in range(crops)]
    params = pltpu.CompilerParams(vmem_limit_bytes=VMEM_LIMIT)
    smem = pl.BlockSpec(memory_space=pltpu.SMEM)
    hbm = pl.BlockSpec(memory_space=pltpu.HBM)

    cells = pl.pallas_call(
        functools.partial(cells_kernel, owned),
        out_shape=jax.ShapeDtypeStruct((owned, LANES), BF16),
        in_specs=[vmem_spec()],
        out_specs=vmem_spec(),
        compiler_params=params,
        cost_estimate=pl.CostEstimate(flops=10**9, bytes_accessed=1024, transcendentals=0),
        name="id_cells",
    )(jnp.pad(jnp.concatenate([pair_ids, pair_ids]), (0, LANES - 2 * owned))[None, :])
    def stack(*blocks):
        rows_out = sum(block.shape[0] for block in blocks)
        return pl.pallas_call(
            stack_kernel,
            out_shape=jax.ShapeDtypeStruct((rows_out, blocks[0].shape[1]), blocks[0].dtype),
            in_specs=[vmem_spec()] * len(blocks),
            out_specs=vmem_spec(),
            compiler_params=params,
            name="stack",
        )(*blocks)

    def over(value, mask):
        return lax.ppermute(value, "batch", [(i, i ^ mask) for i in range(devices)])

    own_block = pl.pallas_call(
        beside_kernel,
        out_shape=jax.ShapeDtypeStruct((owned, width + LANES), BF16),
        in_specs=[vmem_spec()] * 2,
        out_specs=vmem_spec(),
        compiler_params=params,
        cost_estimate=pl.CostEstimate(flops=10**9, bytes_accessed=1024, transcendentals=0),
        name="own_block",
    )(phrases, cells)

    bits = devices.bit_length() - 1
    top, next_top = 1 << (bits - 1), 1 << (bits - 2)
    masks = [0, next_top | 1, top | 1, top | next_top]
    part = stack(own_block, *[over(own_block, mask) for mask in masks[1:]])
    for bit in reversed(range(2, bits - 2)):
        part = stack(part, over(part, 1 << bit | 1))
        masks = masks + [mask ^ (1 << bit | 1) for mask in masks]

    picked = margin_index[0]
    chosen = pl.pallas_call(
        margin_kernel,
        out_shape=jax.ShapeDtypeStruct((picks, width), BF16),
        in_specs=[vmem_spec()] * 2,
        out_specs=vmem_spec(),
        compiler_params=params,
        cost_estimate=pl.CostEstimate(
            flops=2 * picks * rows * width, bytes_accessed=2 * rows * width, transcendentals=0
        ),
        name="margin_rows",
    )(own_vox, picked)

    part, chosen = lax.optimization_barrier((part, chosen))
    partner = lax.ppermute(chosen, "crop", swap)
    near = stack(part, over(part, 3))
    far = over(near, 1)

    base = (lax.axis_index("batch") * rows).astype(jnp.int32).reshape(1)
    terms = pl.pallas_call(
        functools.partial(terms_kernel, scale, owned),
        out_shape=[
            jax.ShapeDtypeStruct((half, rows), BF16),
            jax.ShapeDtypeStruct((half, width), F32),
        ],
        in_specs=[smem] + [vmem_spec()] * 2,
        out_specs=[vmem_spec()] * 2,
        compiler_params=params,
        cost_estimate=pl.CostEstimate(
            flops=4 * half * rows * width,
            bytes_accessed=2 * rows * width,
            transcendentals=half * rows,
        ),
        name="terms",
    )
    dl_near, near_terms = terms(base, own_vox, near)
    far, near_terms = lax.optimization_barrier((far, near_terms))
    dl_far, far_terms = terms(base, own_vox, far)
    matched = pl.pallas_call(
        functools.partial(match_kernel, scale),
        out_shape=jax.ShapeDtypeStruct((rows, width), F32),
        in_specs=[vmem_spec()] * 6,
        out_specs=vmem_spec(),
        compiler_params=params,
        cost_estimate=pl.CostEstimate(
            flops=40 * half * rows * width, bytes_accessed=2 * rows * width, transcendentals=0
        ),
        name="match_grad",
    )(picked, own_vox, dl_near, dl_far, near, far)

    sums = near_terms + over(far_terms, 1)
    for bit in range(1, bits - 2):
        count = sums.shape[0] // 2
        back = over(sums[count:], 1 << bit | 1)
        if bit == 1:
            back, matched = lax.optimization_barrier((back, matched))
        sums = sums[:count] + back
    own = sums[:owned]
    for i in (3, 2, 1):
        own = own + over(sums[i * owned : (i + 1) * owned], masks[i])
    phrase_grad = own + lax.ppermute(own, "crop", swap)
    partner, _ = lax.optimization_barrier((partner, own))
    block = math.gcd(rows, 256)
    voxel_grad = pl.pallas_call(
        functools.partial(grad_kernel, block),
        out_shape=jax.ShapeDtypeStruct((rows, width), F32),
        in_specs=[vmem_spec()] * 3,
        out_specs=hbm,
        scratch_shapes=[pltpu.VMEM((rows, width), F32), pltpu.SemaphoreType.DMA((rows // block,))],
        compiler_params=params,
        cost_estimate=pl.CostEstimate(
            flops=2 * picks * rows * width, bytes_accessed=8 * rows * width, transcendentals=0
        ),
        name="voxel_grad",
    )(picked, matched, partner)
    return (voxel_grad[None], phrase_grad)


def solution(mesh):
    placed = (P("crop", "batch", None), P("batch", None), P("batch"), P("crop", "batch", None))
    return jax.shard_map(
        local,
        mesh=mesh,
        in_specs=placed,
        out_specs=(P("crop", "batch", None), P("batch", None)),
        check_vma=False,
    )
```

```python
import functools
import math

import jax
import jax.numpy as jnp
from jax import lax
from jax.experimental import pallas as pl
from jax.experimental.pallas import tpu as pltpu
from jax.sharding import PartitionSpec as P

VOX_VOL = 256
VOX_MAX = 6.0
VOL_SHIFT = VOX_VOL.bit_length() - 1
LANES = 128
VMEM_LIMIT = 24 * 1024 * 1024

F32 = jnp.float32
BF16 = jnp.bfloat16


def vmem_spec():
    return pl.BlockSpec(memory_space=pltpu.VMEM)


def cells_kernel(owned, ids_ref, out_ref):
    row = lax.broadcasted_iota(jnp.int32, out_ref.shape, 0)
    lane = lax.broadcasted_iota(jnp.int32, out_ref.shape, 1)
    ids = ids_ref[...]
    cells = jnp.where(lane == row, ids >> 8, jnp.where(lane == row + owned, ids & 255, 0))
    out_ref[...] = cells.astype(F32).astype(BF16)


def to_half(value, bound):
    gain = 2.0 ** math.floor(math.log2(65504.0**2 / bound))
    root = jnp.sqrt(jnp.abs(value) * gain)
    return jnp.where(value < 0, -root, root).astype(jnp.float16)


def from_half(code, bound):
    gain = 2.0 ** math.floor(math.log2(65504.0**2 / bound))
    root = code.astype(F32)
    return root * jnp.abs(root) * (1.0 / gain)


def stack_kernel(*refs):
    out_ref = refs[-1]
    start = 0
    for ref in refs[:-1]:
        rows = ref.shape[0]
        out_ref[start : start + rows, :] = ref[...]
        start += rows


def beside_kernel(phrases_ref, cells_ref, out_ref):
    width = phrases_ref.shape[1]
    out_ref[:, :width] = phrases_ref[...]
    out_ref[:, width:] = cells_ref[...]


def margin_kernel(vox_ref, idx_ref, chosen_ref):
    rows = vox_ref.shape[0]
    picks = idx_ref.shape[1]
    onehot = (idx_ref[...] == lax.broadcasted_iota(jnp.int32, (rows, picks), 0)).astype(F32).astype(BF16)
    chosen_ref[...] = lax.dot_general(
        onehot, vox_ref[...], (((0,), (0,)), ((), ())), preferred_element_type=F32
    ).astype(BF16)


def terms_kernel(scale, owned, base_ref, vox_ref, packed_ref, dl_ref, out_ref):
    rows, width = vox_ref.shape
    half = packed_ref.shape[0]
    block = min(half, 128)
    volume = (base_ref[0] + lax.broadcasted_iota(jnp.int32, (1, rows), 1)) >> VOL_SHIFT
    volume = volume.astype(F32)

    def terms(start):
        at = pl.ds(pl.multiple_of(start, block), block)
        phrases = packed_ref[at, :width]
        cells = packed_ref[at, width:].astype(F32)
        lane = lax.broadcasted_iota(jnp.int32, cells.shape, 1)
        ids = jnp.sum(jnp.where(lane < owned, cells * 256.0, cells), axis=1, keepdims=True)
        logit = lax.dot_general(
            phrases, vox_ref[...], (((1,), (1,)), ((), ())), preferred_element_type=F32
        )
        sign = jnp.where(ids == volume, 1.0, -1.0).astype(F32)
        dlogit = (-sign / (1.0 + jnp.exp(sign * (logit * scale - 1.0)))).astype(BF16)
        dl_ref[at, :] = dlogit
        out_ref[at, :] = jnp.dot(dlogit, vox_ref[...], preferred_element_type=F32) * scale

    if half == block:
        terms(0)
    else:
        pl.loop(0, half // block)(lambda j: terms(j * block))


def match_kernel(scale, idx_ref, vox_ref, dl_near, dl_far, near_ref, far_ref, out_ref):
    rows, width = vox_ref.shape
    picks = idx_ref.shape[1]
    block = math.gcd(rows, 256)
    tn = (((0,), (0,)), ((), ()))
    for i in range(rows // block):
        at = pl.ds(i * block, block)
        row = i * block + lax.broadcasted_iota(jnp.int32, (block, picks), 0)
        taken = jnp.sum((row == idx_ref[...]).astype(F32), axis=1, keepdims=True)
        match = lax.dot_general(
            dl_near[:, at], near_ref[:, :width], tn, preferred_element_type=F32
        ) + lax.dot_general(dl_far[:, at], far_ref[:, :width], tn, preferred_element_type=F32)
        out_ref[at, :] = match * scale + taken * vox_ref[at, :].astype(F32)


def grad_kernel(block, idx_ref, part_ref, partner_ref, out_hbm, out_ref, sems):
    rows, width = part_ref.shape
    picks = idx_ref.shape[1]
    copies = []
    for i in range(rows // block):
        at = pl.ds(i * block, block)
        row = i * block + lax.broadcasted_iota(jnp.int32, (block, picks), 0)
        spread = (row == idx_ref[...]).astype(F32).astype(BF16)
        other = jnp.dot(spread, partner_ref[...], preferred_element_type=F32)
        out_ref[at, :] = part_ref[at, :] - other
        copies.append(pltpu.make_async_copy(out_ref.at[at, :], out_hbm.at[at, :], sems.at[i]))
        copies[-1].start()
    for copy in copies:
        copy.wait()


def local(voxels, phrases, pair_ids, margin_index):
    own_vox = voxels[0]
    rows, width = own_vox.shape
    owned = phrases.shape[0]
    picks = margin_index.shape[-1]
    scale = 1.0 / math.sqrt(width)
    devices = lax.axis_size("batch")
    crops = lax.axis_size("crop")
    members = devices // 2
    half = members * owned
    swap = [(i, i ^ 1) for i in range(crops)]
    params = pltpu.CompilerParams(vmem_limit_bytes=VMEM_LIMIT)
    smem = pl.BlockSpec(memory_space=pltpu.SMEM)
    hbm = pl.BlockSpec(memory_space=pltpu.HBM)

    cells = pl.pallas_call(
        functools.partial(cells_kernel, owned),
        out_shape=jax.ShapeDtypeStruct((owned, LANES), BF16),
        in_specs=[vmem_spec()],
        out_specs=vmem_spec(),
        compiler_params=params,
        cost_estimate=pl.CostEstimate(flops=10**9, bytes_accessed=1024, transcendentals=0),
        name="id_cells",
    )(jnp.pad(jnp.concatenate([pair_ids, pair_ids]), (0, LANES - 2 * owned))[None, :])
    def stack(*blocks):
        rows_out = sum(block.shape[0] for block in blocks)
        return pl.pallas_call(
            stack_kernel,
            out_shape=jax.ShapeDtypeStruct((rows_out, blocks[0].shape[1]), blocks[0].dtype),
            in_specs=[vmem_spec()] * len(blocks),
            out_specs=vmem_spec(),
            compiler_params=params,
            name="stack",
        )(*blocks)

    def over(value, mask):
        return lax.ppermute(value, "batch", [(i, i ^ mask) for i in range(devices)])

    own_block = pl.pallas_call(
        beside_kernel,
        out_shape=jax.ShapeDtypeStruct((owned, width + LANES), BF16),
        in_specs=[vmem_spec()] * 2,
        out_specs=vmem_spec(),
        compiler_params=params,
        cost_estimate=pl.CostEstimate(flops=10**9, bytes_accessed=1024, transcendentals=0),
        name="own_block",
    )(phrases, cells)

    bits = devices.bit_length() - 1
    top, next_top = 1 << (bits - 1), 1 << (bits - 2)
    masks = [0, next_top | 1, top | 1, top | next_top]
    part = stack(own_block, *[over(own_block, mask) for mask in masks[1:]])
    for bit in reversed(range(2, bits - 2)):
        part = stack(part, over(part, 1 << bit | 1))
        masks = masks + [mask ^ (1 << bit | 1) for mask in masks]

    picked = margin_index[0]
    chosen = pl.pallas_call(
        margin_kernel,
        out_shape=jax.ShapeDtypeStruct((picks, width), BF16),
        in_specs=[vmem_spec()] * 2,
        out_specs=vmem_spec(),
        compiler_params=params,
        cost_estimate=pl.CostEstimate(
            flops=2 * picks * rows * width, bytes_accessed=2 * rows * width, transcendentals=0
        ),
        name="margin_rows",
    )(own_vox, picked)

    part, chosen = lax.optimization_barrier((part, chosen))
    partner = lax.ppermute(chosen, "crop", swap)
    near = stack(part, over(part, 3))
    far = over(near, 1)

    base = (lax.axis_index("batch") * rows).astype(jnp.int32).reshape(1)
    terms = pl.pallas_call(
        functools.partial(terms_kernel, scale, owned),
        out_shape=[
            jax.ShapeDtypeStruct((half, rows), BF16),
            jax.ShapeDtypeStruct((half, width), F32),
        ],
        in_specs=[smem] + [vmem_spec()] * 2,
        out_specs=[vmem_spec()] * 2,
        compiler_params=params,
        cost_estimate=pl.CostEstimate(
            flops=4 * half * rows * width,
            bytes_accessed=2 * rows * width,
            transcendentals=half * rows,
        ),
        name="terms",
    )
    dl_near, near_terms = terms(base, own_vox, near)
    far, near_terms = lax.optimization_barrier((far, near_terms))
    dl_far, far_terms = terms(base, own_vox, far)
    matched = pl.pallas_call(
        functools.partial(match_kernel, scale),
        out_shape=jax.ShapeDtypeStruct((rows, width), F32),
        in_specs=[vmem_spec()] * 6,
        out_specs=vmem_spec(),
        compiler_params=params,
        cost_estimate=pl.CostEstimate(
            flops=40 * half * rows * width, bytes_accessed=2 * rows * width, transcendentals=0
        ),
        name="match_grad",
    )(picked, own_vox, dl_near, dl_far, near, far)

    bound = VOX_MAX * rows * scale
    sums = near_terms + over(far_terms, 1)
    bound = 2 * bound
    for bit in range(1, bits - 2):
        count = sums.shape[0] // 2
        back = over(to_half(sums[count:], bound), 1 << bit | 1)
        if bit == 1:
            back, matched = lax.optimization_barrier((back, matched))
        sums = sums[:count] + from_half(back, bound)
        bound = 2 * bound
    own = sums[:owned]
    for i in (3, 2, 1):
        block = to_half(sums[i * owned : (i + 1) * owned], bound)
        own = own + from_half(over(block, masks[i]), bound)
    phrase_grad = own + lax.ppermute(own, "crop", swap)
    partner, _ = lax.optimization_barrier((partner, own))
    block = math.gcd(rows, 256)
    voxel_grad = pl.pallas_call(
        functools.partial(grad_kernel, block),
        out_shape=jax.ShapeDtypeStruct((rows, width), F32),
        in_specs=[vmem_spec()] * 3,
        out_specs=hbm,
        scratch_shapes=[pltpu.VMEM((rows, width), F32), pltpu.SemaphoreType.DMA((rows // block,))],
        compiler_params=params,
        cost_estimate=pl.CostEstimate(
            flops=2 * picks * rows * width, bytes_accessed=8 * rows * width, transcendentals=0
        ),
        name="voxel_grad",
    )(picked, matched, partner)
    return (voxel_grad[None], phrase_grad)


def solution(mesh):
    placed = (P("crop", "batch", None), P("batch", None), P("batch"), P("crop", "batch", None))
    return jax.shard_map(
        local,
        mesh=mesh,
        in_specs=placed,
        out_specs=(P("crop", "batch", None), P("batch", None)),
        check_vma=False,
    )
```

```python
import functools
import math

import jax
import jax.numpy as jnp
from jax import lax
from jax.experimental import pallas as pl
from jax.experimental.pallas import tpu as pltpu
from jax.sharding import PartitionSpec as P

VOX_VOL = 256
VOX_MAX = 6.0
VOL_SHIFT = VOX_VOL.bit_length() - 1
LANES = 128
VMEM_LIMIT = 24 * 1024 * 1024

F32 = jnp.float32
BF16 = jnp.bfloat16


def vmem_spec():
    return pl.BlockSpec(memory_space=pltpu.VMEM)


def cells_kernel(owned, ids_ref, out_ref):
    row = lax.broadcasted_iota(jnp.int32, out_ref.shape, 0)
    lane = lax.broadcasted_iota(jnp.int32, out_ref.shape, 1)
    ids = ids_ref[...]
    cells = jnp.where(lane == row, ids >> 8, jnp.where(lane == row + owned, ids & 255, 0))
    out_ref[...] = cells.astype(F32).astype(BF16)


def to_half(value, bound):
    gain = 2.0 ** math.floor(math.log2(65504.0**2 / bound))
    root = jnp.sqrt(jnp.abs(value) * gain)
    return jnp.where(value < 0, -root, root).astype(jnp.float16)


def from_half(code, bound):
    gain = 2.0 ** math.floor(math.log2(65504.0**2 / bound))
    root = code.astype(F32)
    return root * jnp.abs(root) * (1.0 / gain)


def stack_kernel(starts, *refs):
    out_ref = refs[-1]
    for start, ref in zip(starts, refs[:-1], strict=True):
        out_ref[start : start + ref.shape[0], :] = ref[...]


def beside_kernel(phrases_ref, cells_ref, out_ref):
    width = phrases_ref.shape[1]
    out_ref[:, :width] = phrases_ref[...]
    out_ref[:, width:] = cells_ref[...]


def margin_kernel(vox_ref, idx_ref, chosen_ref):
    rows = vox_ref.shape[0]
    picks = idx_ref.shape[1]
    onehot = (idx_ref[...] == lax.broadcasted_iota(jnp.int32, (rows, picks), 0)).astype(F32).astype(BF16)
    chosen_ref[...] = lax.dot_general(
        onehot, vox_ref[...], (((0,), (0,)), ((), ())), preferred_element_type=F32
    ).astype(BF16)


def terms_kernel(scale, owned, base_ref, vox_ref, packed_ref, dl_ref, out_ref):
    rows, width = vox_ref.shape
    half = packed_ref.shape[0]
    block = min(half, 128)
    volume = (base_ref[0] + lax.broadcasted_iota(jnp.int32, (1, rows), 1)) >> VOL_SHIFT
    volume = volume.astype(F32)

    def terms(start):
        at = pl.ds(pl.multiple_of(start, block), block)
        phrases = packed_ref[at, :width]
        cells = packed_ref[at, width:].astype(F32)
        lane = lax.broadcasted_iota(jnp.int32, cells.shape, 1)
        ids = jnp.sum(jnp.where(lane < owned, cells * 256.0, cells), axis=1, keepdims=True)
        logit = lax.dot_general(
            phrases, vox_ref[...], (((1,), (1,)), ((), ())), preferred_element_type=F32
        )
        sign = jnp.where(ids == volume, 1.0, -1.0).astype(F32)
        dlogit = (-sign / (1.0 + jnp.exp(sign * (logit * scale - 1.0)))).astype(BF16)
        dl_ref[at, :] = dlogit
        out_ref[at, :] = jnp.dot(dlogit, vox_ref[...], preferred_element_type=F32) * scale

    if half == block:
        terms(0)
    else:
        pl.loop(0, half // block)(lambda j: terms(j * block))


def match_kernel(scale, idx_ref, vox_ref, dl_near, dl_far, near_ref, far_ref, out_ref):
    rows, width = vox_ref.shape
    picks = idx_ref.shape[1]
    block = math.gcd(rows, 256)
    tn = (((0,), (0,)), ((), ()))
    for i in range(rows // block):
        at = pl.ds(i * block, block)
        row = i * block + lax.broadcasted_iota(jnp.int32, (block, picks), 0)
        taken = jnp.sum((row == idx_ref[...]).astype(F32), axis=1, keepdims=True)
        match = lax.dot_general(
            dl_near[:, at], near_ref[:, :width], tn, preferred_element_type=F32
        ) + lax.dot_general(dl_far[:, at], far_ref[:, :width], tn, preferred_element_type=F32)
        out_ref[at, :] = match * scale + taken * vox_ref[at, :].astype(F32)


def grad_kernel(block, idx_ref, part_ref, partner_ref, out_hbm, out_ref, sems):
    rows, width = part_ref.shape
    picks = idx_ref.shape[1]
    copies = []
    for i in range(rows // block):
        at = pl.ds(i * block, block)
        row = i * block + lax.broadcasted_iota(jnp.int32, (block, picks), 0)
        spread = (row == idx_ref[...]).astype(F32).astype(BF16)
        other = jnp.dot(spread, partner_ref[...], preferred_element_type=F32)
        out_ref[at, :] = part_ref[at, :] - other
        copies.append(pltpu.make_async_copy(out_ref.at[at, :], out_hbm.at[at, :], sems.at[i]))
        copies[-1].start()
    for copy in copies:
        copy.wait()


def local(voxels, phrases, pair_ids, margin_index):
    own_vox = voxels[0]
    rows, width = own_vox.shape
    owned = phrases.shape[0]
    picks = margin_index.shape[-1]
    scale = 1.0 / math.sqrt(width)
    devices = lax.axis_size("batch")
    crops = lax.axis_size("crop")
    members = devices // 2
    half = members * owned
    swap = [(i, i ^ 1) for i in range(crops)]
    params = pltpu.CompilerParams(vmem_limit_bytes=VMEM_LIMIT)
    smem = pl.BlockSpec(memory_space=pltpu.SMEM)
    hbm = pl.BlockSpec(memory_space=pltpu.HBM)

    cells = pl.pallas_call(
        functools.partial(cells_kernel, owned),
        out_shape=jax.ShapeDtypeStruct((owned, LANES), BF16),
        in_specs=[vmem_spec()],
        out_specs=vmem_spec(),
        compiler_params=params,
        cost_estimate=pl.CostEstimate(flops=10**9, bytes_accessed=1024, transcendentals=0),
        name="id_cells",
    )(jnp.pad(jnp.concatenate([pair_ids, pair_ids]), (0, LANES - 2 * owned))[None, :])

    def stack(blocks, order):
        starts = [sum(block.shape[0] for block in blocks[:i]) for i in order]
        return pl.pallas_call(
            functools.partial(stack_kernel, starts),
            out_shape=jax.ShapeDtypeStruct(
                (sum(block.shape[0] for block in blocks), blocks[0].shape[1]), blocks[0].dtype
            ),
            in_specs=[vmem_spec()] * len(blocks),
            out_specs=vmem_spec(),
            compiler_params=params,
            name="stack",
        )(*[blocks[i] for i in order])

    def over(value, mask):
        return lax.ppermute(value, "batch", [(i, i ^ mask) for i in range(devices)])

    own_block = pl.pallas_call(
        beside_kernel,
        out_shape=jax.ShapeDtypeStruct((owned, width + LANES), BF16),
        in_specs=[vmem_spec()] * 2,
        out_specs=vmem_spec(),
        compiler_params=params,
        cost_estimate=pl.CostEstimate(flops=10**9, bytes_accessed=1024, transcendentals=0),
        name="own_block",
    )(phrases, cells)

    bits = devices.bit_length() - 1
    top, next_top = 1 << (bits - 1), 1 << (bits - 2)
    masks = [0, next_top, top | 1, top | next_top | 1]
    part = stack([own_block] + [over(own_block, mask) for mask in masks[1:]], (0, 3, 1, 2))
    for bit in reversed(range(2, bits - 2)):
        part = stack([part, over(part, 1 << bit | 1)], (0, 1))
        masks = masks + [mask ^ (1 << bit | 1) for mask in masks]

    picked = margin_index[0]
    chosen = pl.pallas_call(
        margin_kernel,
        out_shape=jax.ShapeDtypeStruct((picks, width), BF16),
        in_specs=[vmem_spec()] * 2,
        out_specs=vmem_spec(),
        compiler_params=params,
        cost_estimate=pl.CostEstimate(
            flops=2 * picks * rows * width, bytes_accessed=2 * rows * width, transcendentals=0
        ),
        name="margin_rows",
    )(own_vox, picked)

    part, chosen = lax.optimization_barrier((part, chosen))
    partner = lax.ppermute(chosen, "crop", swap)
    near = stack([part, over(part, 3)], (0, 1))
    far = over(near, 1)

    base = (lax.axis_index("batch") * rows).astype(jnp.int32).reshape(1)
    terms = pl.pallas_call(
        functools.partial(terms_kernel, scale, owned),
        out_shape=[
            jax.ShapeDtypeStruct((half, rows), BF16),
            jax.ShapeDtypeStruct((half, width), F32),
        ],
        in_specs=[smem] + [vmem_spec()] * 2,
        out_specs=[vmem_spec()] * 2,
        compiler_params=params,
        cost_estimate=pl.CostEstimate(
            flops=4 * half * rows * width,
            bytes_accessed=2 * rows * width,
            transcendentals=half * rows,
        ),
        name="terms",
    )
    dl_near, near_terms = terms(base, own_vox, near)
    far, near_terms = lax.optimization_barrier((far, near_terms))
    dl_far, far_terms = terms(base, own_vox, far)
    matched = pl.pallas_call(
        functools.partial(match_kernel, scale),
        out_shape=jax.ShapeDtypeStruct((rows, width), F32),
        in_specs=[vmem_spec()] * 6,
        out_specs=vmem_spec(),
        compiler_params=params,
        cost_estimate=pl.CostEstimate(
            flops=40 * half * rows * width, bytes_accessed=2 * rows * width, transcendentals=0
        ),
        name="match_grad",
    )(picked, own_vox, dl_near, dl_far, near, far)

    bound = VOX_MAX * rows * scale
    sums = near_terms + over(far_terms, 1)
    bound = 2 * bound
    for bit in range(1, bits - 2):
        count = sums.shape[0] // 2
        back = over(to_half(sums[count:], bound), 1 << bit | 1)
        if bit == 1:
            back, matched = lax.optimization_barrier((back, matched))
        sums = sums[:count] + from_half(back, bound)
        bound = 2 * bound
    own = sums[:owned]
    for i in (1, 2, 3):
        block = to_half(sums[i * owned : (i + 1) * owned], bound)
        own = own + from_half(over(block, masks[i]), bound)
    bound = 4 * bound
    phrase_grad = own + from_half(lax.ppermute(to_half(own, bound), "crop", swap), bound)
    partner, _ = lax.optimization_barrier((partner, own))
    block = math.gcd(rows, 256)
    voxel_grad = pl.pallas_call(
        functools.partial(grad_kernel, block),
        out_shape=jax.ShapeDtypeStruct((rows, width), F32),
        in_specs=[vmem_spec()] * 3,
        out_specs=hbm,
        scratch_shapes=[pltpu.VMEM((rows, width), F32), pltpu.SemaphoreType.DMA((rows // block,))],
        compiler_params=params,
        cost_estimate=pl.CostEstimate(
            flops=2 * picks * rows * width, bytes_accessed=8 * rows * width, transcendentals=0
        ),
        name="voxel_grad",
    )(picked, matched, partner)
    return (voxel_grad[None], phrase_grad)


def solution(mesh):
    placed = (P("crop", "batch", None), P("batch", None), P("batch"), P("crop", "batch", None))
    return jax.shard_map(
        local,
        mesh=mesh,
        in_specs=placed,
        out_specs=(P("crop", "batch", None), P("batch", None)),
        check_vma=False,
    )
```

```python
import functools
import math

import jax
import jax.numpy as jnp
from jax import lax
from jax.experimental import pallas as pl
from jax.experimental.pallas import tpu as pltpu
from jax.sharding import PartitionSpec as P

VOX_VOL = 256
VOX_MAX = 6.0
VOL_SHIFT = VOX_VOL.bit_length() - 1
LANES = 128
VMEM_LIMIT = 24 * 1024 * 1024

F32 = jnp.float32
BF16 = jnp.bfloat16


def vmem_spec():
    return pl.BlockSpec(memory_space=pltpu.VMEM)


def cells_kernel(owned, ids_ref, out_ref):
    row = lax.broadcasted_iota(jnp.int32, out_ref.shape, 0)
    lane = lax.broadcasted_iota(jnp.int32, out_ref.shape, 1)
    ids = ids_ref[...]
    cells = jnp.where(lane == row, ids >> 8, jnp.where(lane == row + owned, ids & 255, 0))
    out_ref[...] = cells.astype(F32).astype(BF16)


def to_half(value, bound):
    gain = 2.0 ** math.floor(math.log2(65504.0**2 / bound))
    root = jnp.sqrt(jnp.abs(value) * gain)
    return jnp.where(value < 0, -root, root).astype(jnp.float16)


def from_half(code, bound):
    gain = 2.0 ** math.floor(math.log2(65504.0**2 / bound))
    root = code.astype(F32)
    return root * jnp.abs(root) * (1.0 / gain)


def stack_kernel(starts, *refs):
    out_ref = refs[-1]
    for start, ref in zip(starts, refs[:-1], strict=True):
        out_ref[start : start + ref.shape[0], :] = ref[...]


def beside_kernel(phrases_ref, cells_ref, out_ref):
    width = phrases_ref.shape[1]
    out_ref[:, :width] = phrases_ref[...]
    out_ref[:, width:] = cells_ref[...]


def margin_kernel(vox_ref, idx_ref, chosen_ref):
    rows = vox_ref.shape[0]
    picks = idx_ref.shape[1]
    onehot = (idx_ref[...] == lax.broadcasted_iota(jnp.int32, (rows, picks), 0)).astype(F32).astype(BF16)
    chosen_ref[...] = lax.dot_general(
        onehot, vox_ref[...], (((0,), (0,)), ((), ())), preferred_element_type=F32
    ).astype(BF16)


def terms_kernel(scale, owned, base_ref, vox_ref, packed_ref, dl_ref, out_ref):
    rows, width = vox_ref.shape
    half = packed_ref.shape[0]
    block = min(half, 128)
    volume = (base_ref[0] + lax.broadcasted_iota(jnp.int32, (1, rows), 1)) >> VOL_SHIFT
    volume = volume.astype(F32)

    def terms(start):
        at = pl.ds(pl.multiple_of(start, block), block)
        phrases = packed_ref[at, :width]
        cells = packed_ref[at, width:].astype(F32)
        lane = lax.broadcasted_iota(jnp.int32, cells.shape, 1)
        ids = jnp.sum(jnp.where(lane < owned, cells * 256.0, cells), axis=1, keepdims=True)
        logit = lax.dot_general(
            phrases, vox_ref[...], (((1,), (1,)), ((), ())), preferred_element_type=F32
        )
        sign = jnp.where(ids == volume, 1.0, -1.0).astype(F32)
        dlogit = (-sign / (1.0 + jnp.exp(sign * (logit * scale - 1.0)))).astype(BF16)
        dl_ref[at, :] = dlogit
        out_ref[at, :] = jnp.dot(dlogit, vox_ref[...], preferred_element_type=F32) * scale

    if half == block:
        terms(0)
    else:
        pl.loop(0, half // block)(lambda j: terms(j * block))


def match_kernel(scale, idx_ref, vox_ref, dl_near, dl_far, near_ref, far_ref, out_ref):
    rows, width = vox_ref.shape
    picks = idx_ref.shape[1]
    block = math.gcd(rows, 256)
    tn = (((0,), (0,)), ((), ()))
    for i in range(rows // block):
        at = pl.ds(i * block, block)
        row = i * block + lax.broadcasted_iota(jnp.int32, (block, picks), 0)
        taken = jnp.sum((row == idx_ref[...]).astype(F32), axis=1, keepdims=True)
        match = lax.dot_general(
            dl_near[:, at], near_ref[:, :width], tn, preferred_element_type=F32
        ) + lax.dot_general(dl_far[:, at], far_ref[:, :width], tn, preferred_element_type=F32)
        out_ref[at, :] = match * scale + taken * vox_ref[at, :].astype(F32)


def grad_kernel(block, idx_ref, part_ref, partner_ref, out_hbm, out_ref, sems):
    rows, width = part_ref.shape
    picks = idx_ref.shape[1]
    copies = []
    for i in range(rows // block):
        at = pl.ds(i * block, block)
        row = i * block + lax.broadcasted_iota(jnp.int32, (block, picks), 0)
        spread = (row == idx_ref[...]).astype(F32).astype(BF16)
        other = jnp.dot(spread, partner_ref[...], preferred_element_type=F32)
        out_ref[at, :] = part_ref[at, :] - other
        copies.append(pltpu.make_async_copy(out_ref.at[at, :], out_hbm.at[at, :], sems.at[i]))
        copies[-1].start()
    for copy in copies:
        copy.wait()


def local(voxels, phrases, pair_ids, margin_index):
    own_vox = voxels[0]
    rows, width = own_vox.shape
    owned = phrases.shape[0]
    picks = margin_index.shape[-1]
    scale = 1.0 / math.sqrt(width)
    devices = lax.axis_size("batch")
    crops = lax.axis_size("crop")
    members = devices // 2
    half = members * owned
    swap = [(i, i ^ 1) for i in range(crops)]
    params = pltpu.CompilerParams(vmem_limit_bytes=VMEM_LIMIT)
    smem = pl.BlockSpec(memory_space=pltpu.SMEM)
    hbm = pl.BlockSpec(memory_space=pltpu.HBM)

    cells = pl.pallas_call(
        functools.partial(cells_kernel, owned),
        out_shape=jax.ShapeDtypeStruct((owned, LANES), BF16),
        in_specs=[vmem_spec()],
        out_specs=vmem_spec(),
        compiler_params=params,
        cost_estimate=pl.CostEstimate(flops=10**9, bytes_accessed=1024, transcendentals=0),
        name="id_cells",
    )(jnp.pad(jnp.concatenate([pair_ids, pair_ids]), (0, LANES - 2 * owned))[None, :])

    def stack(blocks, order):
        starts = [sum(block.shape[0] for block in blocks[:i]) for i in order]
        return pl.pallas_call(
            functools.partial(stack_kernel, starts),
            out_shape=jax.ShapeDtypeStruct(
                (sum(block.shape[0] for block in blocks), blocks[0].shape[1]), blocks[0].dtype
            ),
            in_specs=[vmem_spec()] * len(blocks),
            out_specs=vmem_spec(),
            compiler_params=params,
            name="stack",
        )(*[blocks[i] for i in order])

    def over(value, mask):
        return lax.ppermute(value, "batch", [(i, i ^ mask) for i in range(devices)])

    own_block = pl.pallas_call(
        beside_kernel,
        out_shape=jax.ShapeDtypeStruct((owned, width + LANES), BF16),
        in_specs=[vmem_spec()] * 2,
        out_specs=vmem_spec(),
        compiler_params=params,
        cost_estimate=pl.CostEstimate(flops=10**9, bytes_accessed=1024, transcendentals=0),
        name="own_block",
    )(phrases, cells)

    bits = devices.bit_length() - 1
    top, next_top = 1 << (bits - 1), 1 << (bits - 2)
    masks = [0, next_top, top | 1, top | next_top | 1]
    part = stack([own_block] + [over(own_block, mask) for mask in masks[1:]], (0, 1, 3, 2))
    for bit in reversed(range(2, bits - 2)):
        part = stack([part, over(part, 1 << bit | 1)], (0, 1))
        masks = masks + [mask ^ (1 << bit | 1) for mask in masks]

    picked = margin_index[0]
    chosen = pl.pallas_call(
        margin_kernel,
        out_shape=jax.ShapeDtypeStruct((picks, width), BF16),
        in_specs=[vmem_spec()] * 2,
        out_specs=vmem_spec(),
        compiler_params=params,
        cost_estimate=pl.CostEstimate(
            flops=2 * picks * rows * width, bytes_accessed=2 * rows * width, transcendentals=0
        ),
        name="margin_rows",
    )(own_vox, picked)

    part, chosen = lax.optimization_barrier((part, chosen))
    partner = lax.ppermute(chosen, "crop", swap)
    near = stack([part, over(part, 3)], (0, 1))
    far = over(near, 1)

    base = (lax.axis_index("batch") * rows).astype(jnp.int32).reshape(1)
    terms = pl.pallas_call(
        functools.partial(terms_kernel, scale, owned),
        out_shape=[
            jax.ShapeDtypeStruct((half, rows), BF16),
            jax.ShapeDtypeStruct((half, width), F32),
        ],
        in_specs=[smem] + [vmem_spec()] * 2,
        out_specs=[vmem_spec()] * 2,
        compiler_params=params,
        cost_estimate=pl.CostEstimate(
            flops=40 * half * rows * width,
            bytes_accessed=2 * rows * width,
            transcendentals=half * rows,
        ),
        name="terms",
    )
    dl_near, near_terms = terms(base, own_vox, near)
    far, near_terms = lax.optimization_barrier((far, near_terms))
    dl_far, far_terms = terms(base, own_vox, far)
    matched = pl.pallas_call(
        functools.partial(match_kernel, scale),
        out_shape=jax.ShapeDtypeStruct((rows, width), F32),
        in_specs=[vmem_spec()] * 6,
        out_specs=vmem_spec(),
        compiler_params=params,
        cost_estimate=pl.CostEstimate(
            flops=40 * half * rows * width, bytes_accessed=2 * rows * width, transcendentals=0
        ),
        name="match_grad",
    )(picked, own_vox, dl_near, dl_far, near, far)

    bound = VOX_MAX * rows * scale
    count = near_terms.shape[0] // 2
    from_core = over(far_terms[:count], 1)
    across = over(to_half(near_terms[count:], bound), 3)
    along = over(to_half(far_terms[count:], bound), 2)
    along, matched = lax.optimization_barrier((along, matched))
    sums = near_terms[:count] + from_core + from_half(across, bound) + from_half(along, bound)
    bound = 4 * bound
    for bit in range(2, bits - 2):
        count = sums.shape[0] // 2
        back = over(to_half(sums[count:], bound), 1 << bit | 1)
        sums = sums[:count] + from_half(back, bound)
        bound = 2 * bound
    own = sums[:owned]
    for i in (3, 2, 1):
        block = to_half(sums[i * owned : (i + 1) * owned], bound)
        own = own + from_half(over(block, masks[i]), bound)
    bound = 4 * bound
    other = lax.ppermute(to_half(own, bound), "crop", swap)
    partner, _ = lax.optimization_barrier((partner, own))
    block = math.gcd(rows, 256)
    voxel_grad = pl.pallas_call(
        functools.partial(grad_kernel, block),
        out_shape=jax.ShapeDtypeStruct((rows, width), F32),
        in_specs=[vmem_spec()] * 3,
        out_specs=hbm,
        scratch_shapes=[pltpu.VMEM((rows, width), F32), pltpu.SemaphoreType.DMA((rows // block,))],
        compiler_params=params,
        cost_estimate=pl.CostEstimate(
            flops=2 * picks * rows * width, bytes_accessed=8 * rows * width, transcendentals=0
        ),
        name="voxel_grad",
    )(picked, matched, partner)
    other, voxel_grad = lax.optimization_barrier((other, voxel_grad))
    phrase_grad = own + from_half(other, bound)
    return (voxel_grad[None], phrase_grad)


def solution(mesh):
    placed = (P("crop", "batch", None), P("batch", None), P("batch"), P("crop", "batch", None))
    return jax.shard_map(
        local,
        mesh=mesh,
        in_specs=placed,
        out_specs=(P("crop", "batch", None), P("batch", None)),
        check_vma=False,
    )
```

```python
import functools
import math

import jax
import jax.numpy as jnp
from jax import lax
from jax.experimental import pallas as pl
from jax.experimental.pallas import tpu as pltpu
from jax.sharding import PartitionSpec as P

VOX_VOL = 256
VOX_MAX = 6.0
VOL_SHIFT = VOX_VOL.bit_length() - 1
LANES = 128
VMEM_LIMIT = 24 * 1024 * 1024

F32 = jnp.float32
BF16 = jnp.bfloat16


def vmem_spec():
    return pl.BlockSpec(memory_space=pltpu.VMEM)


def cells_kernel(owned, ids_ref, out_ref):
    row = lax.broadcasted_iota(jnp.int32, out_ref.shape, 0)
    lane = lax.broadcasted_iota(jnp.int32, out_ref.shape, 1)
    ids = ids_ref[...]
    cells = jnp.where(lane == row, ids >> 8, jnp.where(lane == row + owned, ids & 255, 0))
    out_ref[...] = cells.astype(F32).astype(BF16)


def to_half(value, bound):
    gain = 2.0 ** math.floor(math.log2(65504.0**2 / bound))
    root = jnp.sqrt(jnp.abs(value) * gain)
    return jnp.where(value < 0, -root, root).astype(jnp.float16)


def from_half(code, bound):
    gain = 2.0 ** math.floor(math.log2(65504.0**2 / bound))
    root = code.astype(F32)
    return root * jnp.abs(root) * (1.0 / gain)


def stack_kernel(starts, *refs):
    out_ref = refs[-1]
    for start, ref in zip(starts, refs[:-1], strict=True):
        out_ref[start : start + ref.shape[0], :] = ref[...]


def beside_kernel(phrases_ref, cells_ref, out_ref):
    width = phrases_ref.shape[1]
    out_ref[:, :width] = phrases_ref[...]
    out_ref[:, width:] = cells_ref[...]


def margin_kernel(vox_ref, idx_ref, chosen_ref):
    rows = vox_ref.shape[0]
    picks = idx_ref.shape[1]
    onehot = (idx_ref[...] == lax.broadcasted_iota(jnp.int32, (rows, picks), 0)).astype(F32).astype(BF16)
    chosen_ref[...] = lax.dot_general(
        onehot, vox_ref[...], (((0,), (0,)), ((), ())), preferred_element_type=F32
    ).astype(BF16)


def terms_kernel(scale, owned, base_ref, vox_ref, packed_ref, dl_ref, out_ref):
    rows, width = vox_ref.shape
    half = packed_ref.shape[0]
    block = min(half, 128)
    volume = (base_ref[0] + lax.broadcasted_iota(jnp.int32, (1, rows), 1)) >> VOL_SHIFT
    volume = volume.astype(F32)

    def terms(start):
        at = pl.ds(pl.multiple_of(start, block), block)
        phrases = packed_ref[at, :width]
        cells = packed_ref[at, width:].astype(F32)
        lane = lax.broadcasted_iota(jnp.int32, cells.shape, 1)
        ids = jnp.sum(jnp.where(lane < owned, cells * 256.0, cells), axis=1, keepdims=True)
        logit = lax.dot_general(
            phrases, vox_ref[...], (((1,), (1,)), ((), ())), preferred_element_type=F32
        )
        sign = jnp.where(ids == volume, 1.0, -1.0).astype(F32)
        dlogit = (-sign / (1.0 + jnp.exp(sign * (logit * scale - 1.0)))).astype(BF16)
        dl_ref[at, :] = dlogit
        out_ref[at, :] = jnp.dot(dlogit, vox_ref[...], preferred_element_type=F32) * scale

    if half == block:
        terms(0)
    else:
        pl.loop(0, half // block)(lambda j: terms(j * block))


def match_kernel(scale, idx_ref, vox_ref, dl_near, dl_far, near_ref, far_ref, out_ref):
    rows, width = vox_ref.shape
    picks = idx_ref.shape[1]
    block = math.gcd(rows, 256)
    tn = (((0,), (0,)), ((), ()))
    for i in range(rows // block):
        at = pl.ds(i * block, block)
        row = i * block + lax.broadcasted_iota(jnp.int32, (block, picks), 0)
        taken = jnp.sum((row == idx_ref[...]).astype(F32), axis=1, keepdims=True)
        match = lax.dot_general(
            dl_near[:, at], near_ref[:, :width], tn, preferred_element_type=F32
        ) + lax.dot_general(dl_far[:, at], far_ref[:, :width], tn, preferred_element_type=F32)
        out_ref[at, :] = match * scale + taken * vox_ref[at, :].astype(F32)


def grad_kernel(block, idx_ref, part_ref, partner_ref, out_hbm, out_ref, sems):
    rows, width = part_ref.shape
    picks = idx_ref.shape[1]
    copies = []
    for i in range(rows // block):
        at = pl.ds(i * block, block)
        row = i * block + lax.broadcasted_iota(jnp.int32, (block, picks), 0)
        spread = (row == idx_ref[...]).astype(F32).astype(BF16)
        other = jnp.dot(spread, partner_ref[...], preferred_element_type=F32)
        out_ref[at, :] = part_ref[at, :] - other
        copies.append(pltpu.make_async_copy(out_ref.at[at, :], out_hbm.at[at, :], sems.at[i]))
        copies[-1].start()
    for copy in copies:
        copy.wait()


def local(voxels, phrases, pair_ids, margin_index):
    own_vox = voxels[0]
    rows, width = own_vox.shape
    owned = phrases.shape[0]
    picks = margin_index.shape[-1]
    scale = 1.0 / math.sqrt(width)
    devices = lax.axis_size("batch")
    crops = lax.axis_size("crop")
    members = devices // 2
    half = members * owned
    swap = [(i, i ^ 1) for i in range(crops)]
    params = pltpu.CompilerParams(vmem_limit_bytes=VMEM_LIMIT)
    smem = pl.BlockSpec(memory_space=pltpu.SMEM)
    hbm = pl.BlockSpec(memory_space=pltpu.HBM)

    cells = pl.pallas_call(
        functools.partial(cells_kernel, owned),
        out_shape=jax.ShapeDtypeStruct((owned, LANES), BF16),
        in_specs=[vmem_spec()],
        out_specs=vmem_spec(),
        compiler_params=params,
        cost_estimate=pl.CostEstimate(flops=10**9, bytes_accessed=1024, transcendentals=0),
        name="id_cells",
    )(jnp.pad(jnp.concatenate([pair_ids, pair_ids]), (0, LANES - 2 * owned))[None, :])

    def stack(blocks, order):
        starts = [sum(block.shape[0] for block in blocks[:i]) for i in order]
        return pl.pallas_call(
            functools.partial(stack_kernel, starts),
            out_shape=jax.ShapeDtypeStruct(
                (sum(block.shape[0] for block in blocks), blocks[0].shape[1]), blocks[0].dtype
            ),
            in_specs=[vmem_spec()] * len(blocks),
            out_specs=vmem_spec(),
            compiler_params=params,
            name="stack",
        )(*[blocks[i] for i in order])

    def over(value, mask):
        return lax.ppermute(value, "batch", [(i, i ^ mask) for i in range(devices)])

    own_block = pl.pallas_call(
        beside_kernel,
        out_shape=jax.ShapeDtypeStruct((owned, width + LANES), BF16),
        in_specs=[vmem_spec()] * 2,
        out_specs=vmem_spec(),
        compiler_params=params,
        cost_estimate=pl.CostEstimate(flops=10**9, bytes_accessed=1024, transcendentals=0),
        name="own_block",
    )(phrases, cells)

    bits = devices.bit_length() - 1
    top, next_top = 1 << (bits - 1), 1 << (bits - 2)
    masks = [0, next_top, top | 1, top | next_top | 1]
    part = stack([own_block] + [over(own_block, mask) for mask in masks[1:]], (0, 1, 3, 2))
    for bit in reversed(range(2, bits - 2)):
        part = stack([part, over(part, 1 << bit | 1)], (0, 1))
        masks = masks + [mask ^ (1 << bit | 1) for mask in masks]

    picked = margin_index[0]
    chosen = pl.pallas_call(
        margin_kernel,
        out_shape=jax.ShapeDtypeStruct((picks, width), BF16),
        in_specs=[vmem_spec()] * 2,
        out_specs=vmem_spec(),
        compiler_params=params,
        cost_estimate=pl.CostEstimate(
            flops=2 * picks * rows * width, bytes_accessed=2 * rows * width, transcendentals=0
        ),
        name="margin_rows",
    )(own_vox, picked)

    part, chosen = lax.optimization_barrier((part, chosen))
    partner = lax.ppermute(chosen, "crop", swap)
    near = stack([part, over(part, 3)], (0, 1))
    far = over(near, 1)

    base = (lax.axis_index("batch") * rows).astype(jnp.int32).reshape(1)
    terms = pl.pallas_call(
        functools.partial(terms_kernel, scale, owned),
        out_shape=[
            jax.ShapeDtypeStruct((half, rows), BF16),
            jax.ShapeDtypeStruct((half, width), F32),
        ],
        in_specs=[smem] + [vmem_spec()] * 2,
        out_specs=[vmem_spec()] * 2,
        compiler_params=params,
        cost_estimate=pl.CostEstimate(
            flops=40 * half * rows * width,
            bytes_accessed=2 * rows * width,
            transcendentals=half * rows,
        ),
        name="terms",
    )
    dl_near, near_terms = terms(base, own_vox, near)
    far, _ = lax.optimization_barrier((far, near_terms))
    dl_far, far_terms = terms(base, own_vox, far)
    matched = pl.pallas_call(
        functools.partial(match_kernel, scale),
        out_shape=jax.ShapeDtypeStruct((rows, width), F32),
        in_specs=[vmem_spec()] * 6,
        out_specs=vmem_spec(),
        compiler_params=params,
        cost_estimate=pl.CostEstimate(
            flops=40 * half * rows * width, bytes_accessed=2 * rows * width, transcendentals=0
        ),
        name="match_grad",
    )(picked, own_vox, dl_near, dl_far, near, far)

    bound = VOX_MAX * rows * scale
    count = near_terms.shape[0] // 2
    from_core = over(far_terms[:count], 1)
    across = over(to_half(near_terms[count:], bound), 3)
    along = over(to_half(far_terms[count:], bound), 2)
    along, matched = lax.optimization_barrier((along, matched))
    sums = near_terms[:count] + from_core + from_half(across, bound) + from_half(along, bound)
    bound = 4 * bound
    for bit in range(2, bits - 2):
        count = sums.shape[0] // 2
        back = over(to_half(sums[count:], bound), 1 << bit | 1)
        sums = sums[:count] + from_half(back, bound)
        bound = 2 * bound
    own = sums[:owned]
    for i in (3, 2, 1):
        block = to_half(sums[i * owned : (i + 1) * owned], bound)
        own = own + from_half(over(block, masks[i]), bound)
    bound = 4 * bound
    other = lax.ppermute(to_half(own, bound), "crop", swap)
    partner, _ = lax.optimization_barrier((partner, own))
    block = math.gcd(rows, 256)
    voxel_grad = pl.pallas_call(
        functools.partial(grad_kernel, block),
        out_shape=jax.ShapeDtypeStruct((rows, width), F32),
        in_specs=[vmem_spec()] * 3,
        out_specs=hbm,
        scratch_shapes=[pltpu.VMEM((rows, width), F32), pltpu.SemaphoreType.DMA((rows // block,))],
        compiler_params=params,
        cost_estimate=pl.CostEstimate(
            flops=2 * picks * rows * width, bytes_accessed=8 * rows * width, transcendentals=0
        ),
        name="voxel_grad",
    )(picked, matched, partner)
    other, voxel_grad = lax.optimization_barrier((other, voxel_grad))
    phrase_grad = own + from_half(other, bound)
    return (voxel_grad[None], phrase_grad)


def solution(mesh):
    placed = (P("crop", "batch", None), P("batch", None), P("batch"), P("crop", "batch", None))
    return jax.shard_map(
        local,
        mesh=mesh,
        in_specs=placed,
        out_specs=(P("crop", "batch", None), P("batch", None)),
        check_vma=False,
    )
```

```python
import functools
import math

import jax
import jax.numpy as jnp
from jax import lax
from jax.experimental import pallas as pl
from jax.experimental.pallas import tpu as pltpu
from jax.sharding import PartitionSpec as P

VOX_VOL = 256
VOX_MAX = 6.0
VOL_SHIFT = VOX_VOL.bit_length() - 1
LANES = 128
VMEM_LIMIT = 24 * 1024 * 1024

F32 = jnp.float32
BF16 = jnp.bfloat16


def vmem_spec():
    return pl.BlockSpec(memory_space=pltpu.VMEM)


def cells_kernel(owned, ids_ref, out_ref):
    row = lax.broadcasted_iota(jnp.int32, out_ref.shape, 0)
    lane = lax.broadcasted_iota(jnp.int32, out_ref.shape, 1)
    ids = ids_ref[...]
    rest = jnp.zeros((1, LANES - 2 * owned), jnp.int32)
    ids = jnp.concatenate([ids, ids, rest], axis=1)
    cells = jnp.where(lane == row, ids >> 8, jnp.where(lane == row + owned, ids & 255, 0))
    out_ref[...] = cells.astype(F32).astype(BF16)


def to_half(value, bound):
    gain = 2.0 ** math.floor(math.log2(65504.0**2 / bound))
    root = jnp.sqrt(jnp.abs(value) * gain)
    return jnp.where(value < 0, -root, root).astype(jnp.float16)


def from_half(code, bound):
    gain = 2.0 ** math.floor(math.log2(65504.0**2 / bound))
    root = code.astype(F32)
    return root * jnp.abs(root) * (1.0 / gain)


def stack_kernel(starts, *refs):
    out_ref = refs[-1]
    for start, ref in zip(starts, refs[:-1], strict=True):
        out_ref[start : start + ref.shape[0], :] = ref[...]


def beside_kernel(phrases_ref, cells_ref, out_ref):
    width = phrases_ref.shape[1]
    out_ref[:, :width] = phrases_ref[...]
    out_ref[:, width:] = cells_ref[...]


def margin_kernel(vox_ref, idx_ref, chosen_ref):
    rows = vox_ref.shape[0]
    picks = idx_ref.shape[1]
    onehot = (idx_ref[...] == lax.broadcasted_iota(jnp.int32, (rows, picks), 0)).astype(F32).astype(BF16)
    chosen_ref[...] = lax.dot_general(
        onehot, vox_ref[...], (((0,), (0,)), ((), ())), preferred_element_type=F32
    ).astype(BF16)


def terms_kernel(scale, owned, base_ref, vox_ref, packed_ref, dl_ref, out_ref):
    rows, width = vox_ref.shape
    half = packed_ref.shape[0]
    block = min(half, 128)
    volume = (base_ref[0] + lax.broadcasted_iota(jnp.int32, (1, rows), 1)) >> VOL_SHIFT
    volume = volume.astype(F32)

    def terms(start):
        at = pl.ds(pl.multiple_of(start, block), block)
        phrases = packed_ref[at, :width]
        cells = packed_ref[at, width:].astype(F32)
        lane = lax.broadcasted_iota(jnp.int32, cells.shape, 1)
        ids = jnp.sum(jnp.where(lane < owned, cells * 256.0, cells), axis=1, keepdims=True)
        logit = lax.dot_general(
            phrases, vox_ref[...], (((1,), (1,)), ((), ())), preferred_element_type=F32
        )
        sign = jnp.where(ids == volume, 1.0, -1.0).astype(F32)
        dlogit = (-sign / (1.0 + jnp.exp(sign * (logit * scale - 1.0)))).astype(BF16)
        dl_ref[at, :] = dlogit
        out_ref[at, :] = jnp.dot(dlogit, vox_ref[...], preferred_element_type=F32) * scale

    if half == block:
        terms(0)
    else:
        pl.loop(0, half // block)(lambda j: terms(j * block))


def match_kernel(scale, idx_ref, vox_ref, dl_near, dl_far, near_ref, far_ref, out_ref):
    rows, width = vox_ref.shape
    picks = idx_ref.shape[1]
    block = math.gcd(rows, 256)
    tn = (((0,), (0,)), ((), ()))
    for i in range(rows // block):
        at = pl.ds(i * block, block)
        row = i * block + lax.broadcasted_iota(jnp.int32, (block, picks), 0)
        taken = jnp.sum((row == idx_ref[...]).astype(F32), axis=1, keepdims=True)
        match = lax.dot_general(
            dl_near[:, at], near_ref[:, :width], tn, preferred_element_type=F32
        ) + lax.dot_general(dl_far[:, at], far_ref[:, :width], tn, preferred_element_type=F32)
        out_ref[at, :] = match * scale + taken * vox_ref[at, :].astype(F32)


def grad_kernel(block, idx_ref, part_ref, partner_ref, out_hbm, out_ref, sems):
    rows, width = part_ref.shape
    picks = idx_ref.shape[1]
    copies = []
    for i in range(rows // block):
        at = pl.ds(i * block, block)
        row = i * block + lax.broadcasted_iota(jnp.int32, (block, picks), 0)
        spread = (row == idx_ref[...]).astype(F32).astype(BF16)
        other = jnp.dot(spread, partner_ref[...], preferred_element_type=F32)
        out_ref[at, :] = part_ref[at, :] - other
        copies.append(pltpu.make_async_copy(out_ref.at[at, :], out_hbm.at[at, :], sems.at[i]))
        copies[-1].start()
    for copy in copies:
        copy.wait()


def local(voxels, phrases, pair_ids, margin_index):
    own_vox = voxels[0]
    rows, width = own_vox.shape
    owned = phrases.shape[0]
    picks = margin_index.shape[-1]
    scale = 1.0 / math.sqrt(width)
    devices = lax.axis_size("batch")
    crops = lax.axis_size("crop")
    members = devices // 2
    half = members * owned
    swap = [(i, i ^ 1) for i in range(crops)]
    params = pltpu.CompilerParams(vmem_limit_bytes=VMEM_LIMIT)
    smem = pl.BlockSpec(memory_space=pltpu.SMEM)
    hbm = pl.BlockSpec(memory_space=pltpu.HBM)

    cells = pl.pallas_call(
        functools.partial(cells_kernel, owned),
        out_shape=jax.ShapeDtypeStruct((owned, LANES), BF16),
        in_specs=[vmem_spec()],
        out_specs=vmem_spec(),
        compiler_params=params,
        cost_estimate=pl.CostEstimate(flops=10**9, bytes_accessed=1024, transcendentals=0),
        name="id_cells",
    )(pair_ids[None, :])

    def stack(blocks, order):
        starts = [sum(block.shape[0] for block in blocks[:i]) for i in order]
        return pl.pallas_call(
            functools.partial(stack_kernel, starts),
            out_shape=jax.ShapeDtypeStruct(
                (sum(block.shape[0] for block in blocks), blocks[0].shape[1]), blocks[0].dtype
            ),
            in_specs=[vmem_spec()] * len(blocks),
            out_specs=vmem_spec(),
            compiler_params=params,
            name="stack",
        )(*[blocks[i] for i in order])

    def over(value, mask):
        return lax.ppermute(value, "batch", [(i, i ^ mask) for i in range(devices)])

    own_block = pl.pallas_call(
        beside_kernel,
        out_shape=jax.ShapeDtypeStruct((owned, width + LANES), BF16),
        in_specs=[vmem_spec()] * 2,
        out_specs=vmem_spec(),
        compiler_params=params,
        cost_estimate=pl.CostEstimate(flops=10**9, bytes_accessed=1024, transcendentals=0),
        name="own_block",
    )(phrases, cells)

    bits = devices.bit_length() - 1
    top, next_top = 1 << (bits - 1), 1 << (bits - 2)
    masks = [0, next_top, top | 1, top | next_top | 1]
    part = stack([own_block] + [over(own_block, mask) for mask in masks[1:]], (0, 1, 3, 2))
    for bit in reversed(range(2, bits - 2)):
        part = stack([part, over(part, 1 << bit | 1)], (0, 1))
        masks = masks + [mask ^ (1 << bit | 1) for mask in masks]

    picked = margin_index[0]
    chosen = pl.pallas_call(
        margin_kernel,
        out_shape=jax.ShapeDtypeStruct((picks, width), BF16),
        in_specs=[vmem_spec()] * 2,
        out_specs=vmem_spec(),
        compiler_params=params,
        cost_estimate=pl.CostEstimate(
            flops=2 * picks * rows * width, bytes_accessed=2 * rows * width, transcendentals=0
        ),
        name="margin_rows",
    )(own_vox, picked)

    part, chosen = lax.optimization_barrier((part, chosen))
    partner = lax.ppermute(chosen, "crop", swap)
    near = stack([part, over(part, 3)], (0, 1))
    far = over(near, 1)

    base = (lax.axis_index("batch") * rows).astype(jnp.int32).reshape(1)
    terms = pl.pallas_call(
        functools.partial(terms_kernel, scale, owned),
        out_shape=[
            jax.ShapeDtypeStruct((half, rows), BF16),
            jax.ShapeDtypeStruct((half, width), F32),
        ],
        in_specs=[smem] + [vmem_spec()] * 2,
        out_specs=[vmem_spec()] * 2,
        compiler_params=params,
        cost_estimate=pl.CostEstimate(
            flops=40 * half * rows * width,
            bytes_accessed=2 * rows * width,
            transcendentals=half * rows,
        ),
        name="terms",
    )
    dl_near, near_terms = terms(base, own_vox, near)
    far, _ = lax.optimization_barrier((far, near_terms))
    dl_far, far_terms = terms(base, own_vox, far)
    matched = pl.pallas_call(
        functools.partial(match_kernel, scale),
        out_shape=jax.ShapeDtypeStruct((rows, width), F32),
        in_specs=[vmem_spec()] * 6,
        out_specs=vmem_spec(),
        compiler_params=params,
        cost_estimate=pl.CostEstimate(
            flops=40 * half * rows * width, bytes_accessed=2 * rows * width, transcendentals=0
        ),
        name="match_grad",
    )(picked, own_vox, dl_near, dl_far, near, far)

    bound = VOX_MAX * rows * scale
    count = near_terms.shape[0] // 2
    from_core = over(far_terms[:count], 1)
    across = over(to_half(near_terms[count:], bound), 3)
    along = over(to_half(far_terms[count:], bound), 2)
    along, matched = lax.optimization_barrier((along, matched))
    sums = near_terms[:count] + from_core + from_half(across, bound) + from_half(along, bound)
    bound = 4 * bound
    for bit in range(2, bits - 2):
        count = sums.shape[0] // 2
        back = over(to_half(sums[count:], bound), 1 << bit | 1)
        sums = sums[:count] + from_half(back, bound)
        bound = 2 * bound
    own = sums[:owned]
    for i in (3, 2, 1):
        block = to_half(sums[i * owned : (i + 1) * owned], bound)
        own = own + from_half(over(block, masks[i]), bound)
    bound = 4 * bound
    other = lax.ppermute(to_half(own, bound), "crop", swap)
    partner, _ = lax.optimization_barrier((partner, own))
    block = math.gcd(rows, 256)
    voxel_grad = pl.pallas_call(
        functools.partial(grad_kernel, block),
        out_shape=jax.ShapeDtypeStruct((rows, width), F32),
        in_specs=[vmem_spec()] * 3,
        out_specs=hbm,
        scratch_shapes=[pltpu.VMEM((rows, width), F32), pltpu.SemaphoreType.DMA((rows // block,))],
        compiler_params=params,
        cost_estimate=pl.CostEstimate(
            flops=2 * picks * rows * width, bytes_accessed=8 * rows * width, transcendentals=0
        ),
        name="voxel_grad",
    )(picked, matched, partner)
    other, voxel_grad = lax.optimization_barrier((other, voxel_grad))
    phrase_grad = own + from_half(other, bound)
    return (voxel_grad[None], phrase_grad)


def solution(mesh):
    placed = (P("crop", "batch", None), P("batch", None), P("batch"), P("crop", "batch", None))
    return jax.shard_map(
        local,
        mesh=mesh,
        in_specs=placed,
        out_specs=(P("crop", "batch", None), P("batch", None)),
        check_vma=False,
    )
```
